256 devices in a mesh: dp: 8 (over x_lo, y), expert: 32 (over z, x_hi, core).
Axes of the slice: x: 4 (x_hi: 2, x_lo: 2; x = x_hi * 2 + x_lo), y: 4, z: 8, core: 2. Of those that a mesh axis runs over, the one named last changes fastest.
Arguments:
- tokens: bfloat16 [65536, 1280], P(('dp', 'expert')), may hold values from -68 to 68
- router: bfloat16 [1280, 128], replicated, may hold values from -0.5 to 0.5
- expert_in: bfloat16 [64, 1280, 3072], P('expert', None, 'dp'), may hold values from -1.25 to 1.25
- expert_out: bfloat16 [64, 3072, 1280], P('expert', 'dp'), may hold values from -0.625 to 0.625
- cotangent: bfloat16 [65536, 1280], P(('dp', 'expert')), may hold values from -6 to 6
Outputs:
- mixed: bfloat16 [65536, 1280], P(('dp', 'expert'))
- grad_tokens: bfloat16 [65536, 1280], P(('dp', 'expert'))
- grad_router: float32 [1280, 128], replicated
- grad_in: bfloat16 [64, 1280, 3072], P('expert', None, 'dp')
- grad_out: bfloat16 [64, 3072, 1280], P('expert', 'dp')
The draws below stay inside these ranges and needn't reach their ends.
All inputs are finite; a program needn't handle non-finite values.
Results may differ from the reference program's by a relative error of at most 0.023.
Values may be sent and summed in bfloat16 or wider, within the bound.
No kernel may reach another device: no remote copies, remote signals or barrier semaphores. Data moves between devices by JAX's collectives and lax.ppermute only.
A program may use at most 64 MiB of HBM per device.

```python
import math
import jax
import jax.numpy as jnp
from jax import lax

D = 1280
FF = 3072
TOK = 256
SLOTS = 2
EXPERTS = 64
SLOTS_ALL = 128
IMAGES = 256
N_DP = 8


def shared_columns(basekey):
    return jnp.clip(jax.random.normal(basekey, (D, SLOTS_ALL), jnp.float32), -4.0, 4.0)


def draw_router(key, part):
    columns_drawn = shared_columns(key)
    return (columns_drawn / math.sqrt(D)).astype(jnp.bfloat16)


def draw_tokens(key, part):
    key = jax.random.fold_in(key, 7)
    values = jnp.clip(jax.random.normal(key, (IMAGES, TOK, D), jnp.float32), -4.0, 4.0)
    return values.reshape(IMAGES * TOK, D).astype(jnp.bfloat16)


def steps_of(own_key, dims, cuts, least, top_value):
    gain = 1.0
    for position, shards_of in cuts:
        draws = jax.random.uniform(jax.random.fold_in(jax.random.fold_in(own_key, 6), position), (shards_of,), jnp.float32, least / len(cuts), top_value / len(cuts))
        gain = gain * jnp.repeat(jnp.exp(draws), dims[position] // shards_of).reshape((-1,) + (1,) * (len(dims) - 1 - position))
    return gain


def normal_values(rng, shape, width, most, pieces=(), held_as=jnp.bfloat16):
    entries = width * jax.random.normal(rng, shape, jnp.float32)
    if pieces:
        entries = entries * steps_of(rng, shape, pieces, -0.22, 0.18)
    return jnp.clip(entries, -most, most).astype(held_as)


def setup_inputs(seed: int = 0) -> dict:
    keys = jax.random.split(jax.random.key(seed), 6)
    tokens = draw_tokens(jax.random.fold_in(keys[5], 71), 0)
    router = draw_router(jax.random.fold_in(keys[5], 71), 0)
    expert_in = normal_values(keys[2], (EXPERTS, D, FF), (D // 64) ** -0.5, 1.25, ((0, 32), (2, 8)))
    expert_out = normal_values(keys[3], (EXPERTS, FF, D), (FF // 32) ** -0.5, 0.625, ((0, 32), (1, 8)))
    cotangent = normal_values(keys[4], (IMAGES * TOK, D), 1.0, 6.0, ((0, 256),))
    return {"tokens": tokens, "router": router, "expert_in": expert_in, "expert_out": expert_out, "cotangent": cotangent}


def gelu_exact(values):
    return jax.nn.gelu(values, approximate=False)

def grouped_sum(form, left, right):
    parts = jnp.einsum(form, left, right).astype(jnp.bfloat16)
    parts = lax.optimization_barrier(parts).astype(jnp.float32)
    return lax.optimization_barrier(jnp.sum(parts, axis=2)).astype(jnp.bfloat16)

def expert_forward(bundle):
    slot_rows, weight_in, weight_out = bundle
    hidden = jnp.einsum('isd,df->isf', slot_rows.astype(jnp.float32), weight_in.astype(jnp.float32))
    activated = gelu_exact(hidden).astype(jnp.bfloat16)
    act_groups = activated.astype(jnp.float32).reshape(activated.shape[0], activated.shape[1], N_DP, FF // N_DP)
    out_groups = weight_out.astype(jnp.float32).reshape(N_DP, FF // N_DP, D)
    return grouped_sum('isgf,gfd->isgd', act_groups, out_groups)

def expert_backward(bundle):
    slot_rows, grad_rows, weight_in, weight_out = bundle
    hidden = jnp.einsum('isd,df->isf', slot_rows.astype(jnp.float32), weight_in.astype(jnp.float32))
    activated = gelu_exact(hidden).astype(jnp.bfloat16)
    grad_act = jnp.einsum('isd,fd->isf', grad_rows.astype(jnp.float32), weight_out.astype(jnp.float32))
    grad_hidden = jax.vjp(gelu_exact, hidden)[1](grad_act)[0].astype(jnp.bfloat16)
    grad_weight_out = jnp.einsum('isf,isd->fd', activated.astype(jnp.float32), grad_rows.astype(jnp.float32)).astype(jnp.bfloat16)
    grad_weight_in = jnp.einsum('isd,isf->df', slot_rows.astype(jnp.float32), grad_hidden.astype(jnp.float32)).astype(jnp.bfloat16)
    hid_groups = grad_hidden.astype(jnp.float32).reshape(grad_hidden.shape[0], grad_hidden.shape[1], N_DP, FF // N_DP)
    in_groups = weight_in.astype(jnp.float32).reshape(D, N_DP, FF // N_DP)
    grad_slot = grouped_sum('isgf,dgf->isgd', hid_groups, in_groups)
    return (grad_weight_in, grad_weight_out, grad_slot)

def reference(tokens, router, expert_in, expert_out, cotangent):
    images = tokens.reshape(IMAGES, TOK, D).astype(jnp.float32)
    upstream = cotangent.reshape(IMAGES, TOK, D).astype(jnp.float32)
    router_f = router.astype(jnp.float32)
    logits = jnp.einsum('imd,ds->ims', images, router_f)
    dispatch = jax.nn.softmax(logits, axis=1)
    combine = jax.nn.softmax(logits, axis=2)
    dispatch_b = dispatch.astype(jnp.bfloat16).astype(jnp.float32)
    combine_b = combine.astype(jnp.bfloat16).astype(jnp.float32)
    slot_in = jnp.einsum('ims,imd->isd', dispatch_b, images).astype(jnp.bfloat16)
    by_expert = jnp.transpose(slot_in.reshape(IMAGES, EXPERTS, SLOTS, D), (1, 0, 2, 3))
    slot_out_e = lax.map(expert_forward, (by_expert, expert_in, expert_out))
    slot_out = jnp.transpose(slot_out_e, (1, 0, 2, 3)).reshape(IMAGES, SLOTS_ALL, D)
    slot_out_f = slot_out.astype(jnp.float32)
    mixed = jnp.einsum('ims,isd->imd', combine_b, slot_out_f).astype(jnp.bfloat16)
    grad_combine = jnp.einsum('imd,isd->ims', upstream, slot_out_f)
    grad_slot_out = jnp.einsum('ims,imd->isd', combine_b, upstream).astype(jnp.bfloat16)
    logit_combine = combine * (grad_combine - lax.optimization_barrier(jnp.sum(combine * grad_combine, axis=2, keepdims=True)))
    grad_by_expert = jnp.transpose(grad_slot_out.reshape(IMAGES, EXPERTS, SLOTS, D), (1, 0, 2, 3))
    grad_in, grad_out, grad_slot_e = lax.map(expert_backward, (by_expert, grad_by_expert, expert_in, expert_out))
    grad_slot_in = jnp.transpose(grad_slot_e, (1, 0, 2, 3)).reshape(IMAGES, SLOTS_ALL, D).astype(jnp.float32)
    grad_dispatch = jnp.einsum('imd,isd->ims', images, grad_slot_in)
    logit_dispatch = dispatch * (grad_dispatch - lax.optimization_barrier(jnp.sum(dispatch * grad_dispatch, axis=1, keepdims=True)))
    grad_logits = (logit_combine + logit_dispatch).astype(jnp.bfloat16).astype(jnp.float32)
    grad_tokens = jnp.einsum('ims,isd->imd', dispatch_b, grad_slot_in) + jnp.einsum('ims,ds->imd', grad_logits, router_f)
    grad_tokens = grad_tokens.astype(jnp.bfloat16).reshape(IMAGES * TOK, D)
    grad_router = jnp.einsum('imd,ims->ds', images, grad_logits)
    return (mixed.reshape(IMAGES * TOK, D), grad_tokens, grad_router, grad_in, grad_out)
```

```python
import functools
import math

import jax
import jax.numpy as jnp
import numpy as np
from jax import lax
from jax.experimental import pallas as pl
from jax.experimental.pallas import tpu as pltpu
from jax.sharding import Mesh
from jax.sharding import PartitionSpec as P

F32 = jnp.float32
BF16 = jnp.bfloat16
ALL = ("xl", "y", "z", "xh", "c")
DP = ("xl", "y")
EXPERT = ("z", "xh", "c")
PLANE = ("xl", "y", "xh", "c")

PARTS = (((0, 0, 24),), ((1, 0, 24),), ((0, 24, 8), (1, 24, 8)))
ROWS = tuple(sum(4 * n for _, _, n in part) for part in PARTS)
ORDERS = (("x", "y1", "y3"), ("y1", "y3", "x"), ("y3", "x", "y1"))


def row_order():
    order = []
    for part in PARTS:
        for expert, first, count in part:
            for kind in range(2):
                for image in range(first, first + count):
                    for k in range(2):
                        order.append(8 * image + 4 * kind + 2 * expert + k)
    return np.array(order)


def neighbour(dim):
    pairs = []
    for i in range(8):
        x, y = divmod(i, 4)
        if dim == "x":
            x = 1 - x
        elif dim == "y1":
            y = y ^ 1
        else:
            y = 3 - y
        pairs.append((i, x * 4 + y))
    return pairs


def call(kernel, out_shape, args, flops, name):
    shapes = out_shape if isinstance(out_shape, tuple) else (out_shape,)
    moved = sum(math.prod(a.shape) * a.dtype.itemsize for a in tuple(args) + shapes)
    vmem = pl.BlockSpec(memory_space=pltpu.VMEM)
    return pl.pallas_call(
        kernel,
        out_shape=out_shape,
        in_specs=[vmem] * len(args),
        out_specs=(vmem,) * len(shapes) if isinstance(out_shape, tuple) else vmem,
        compiler_params=pltpu.CompilerParams(vmem_limit_bytes=48 * 1024 * 1024),
        cost_estimate=pl.CostEstimate(flops=flops, bytes_accessed=moved, transcendentals=0),
        name=name,
    )(*args)


def dot(a, b, over):
    return lax.dot_general(a, b, (over, ((), ())), preferred_element_type=F32)


PLAIN = ((1,), (0,))
WIDTH = ((1,), (1,))
FIRST = ((0,), (0,))


def spread(slots, wide):
    row = lax.broadcasted_iota(jnp.int32, (slots, wide), 0)
    col = lax.broadcasted_iota(jnp.int32, (slots, wide), 1)
    return (row == 4 * (col // 8) + col % 4).astype(BF16)


def input_columns(shape):
    return lax.broadcasted_iota(jnp.int32, shape, 1) % 8 < 4


def prologue_kernel(tokens, router, cotangent, rows, dispatch_out, combine_out):
    slots = router.shape[1]
    wide = 2 * slots
    router_wide = dot(router[...], spread(slots, wide), PLAIN).astype(BF16)
    logits = dot(tokens[...], router_wide, PLAIN)
    down = jnp.exp(logits - jnp.max(logits, axis=0, keepdims=True))
    dispatch = down / jnp.sum(down, axis=0, keepdims=True)
    across = jnp.exp(logits - jnp.max(logits, axis=1, keepdims=True))
    combine = across / (0.5 * jnp.sum(across, axis=1, keepdims=True))
    inputs = input_columns(logits.shape)
    dispatch_b = jnp.where(inputs, dispatch, 0.0).astype(BF16)
    combine_b = jnp.where(inputs, 0.0, combine).astype(BF16)
    total = dot(dispatch_b, tokens[...], FIRST) + dot(combine_b, cotangent[...], FIRST)
    rows[...] = total.astype(BF16)
    dispatch_out[...] = dispatch
    combine_out[...] = combine


def sort_kernel(order, rows, *parts):
    moved = dot(order[...], rows[...], PLAIN).astype(BF16)
    at = 0
    for part in parts:
        count = part.shape[0]
        part[...] = moved[at : at + count]
        at += count


def unsort_kernel(order, *refs):
    held, received, out = refs[:3], refs[3:6], refs[6]
    total = [
        (a[...].astype(F32) + b[...].astype(F32)).astype(BF16)
        for a, b in zip(held, received, strict=True)
    ]
    out[...] = dot(order[...], jnp.concatenate(total, axis=0), FIRST).astype(BF16)


def gelu_parts(v):
    cdf = 0.5 * (1.0 + lax.erf(v * math.sqrt(0.5)))
    slope = cdf + v * (jnp.exp(-0.5 * v * v) * (1.0 / math.sqrt(2.0 * math.pi)))
    return v * cdf, slope


def expert_kernel(part, blocks, expert_in, expert_out, out, act_out, hid_out):
    count = blocks.shape[0]
    width = blocks.shape[2]
    at = saved = 0
    for expert, _, images in part:
        half = 2 * images
        total = count * half
        rows = blocks[:, at : at + half, :].reshape(total, width)
        grads = blocks[:, at + half : at + 2 * half, :].reshape(total, width)
        hidden = dot(rows, expert_in[expert], PLAIN)
        grad_act = dot(grads, expert_out[expert], WIDTH)
        value, slope = gelu_parts(hidden)
        activated = value.astype(BF16)
        grad_hidden = (slope * grad_act).astype(BF16)
        slot_part = dot(activated, expert_out[expert], PLAIN).astype(BF16)
        grad_part = dot(grad_hidden, expert_in[expert], WIDTH).astype(BF16)
        out[:, at : at + half, :] = slot_part.reshape(count, half, width)
        out[:, at + half : at + 2 * half, :] = grad_part.reshape(count, half, width)
        act_out[saved : saved + total, :] = activated
        hid_out[saved : saved + total, :] = grad_hidden
        at += 2 * half
        saved += total


def weight_kernel(sections, kind, *refs):
    out = refs[-1]
    left, right = [], []
    for i, (at, half, first) in enumerate(sections):
        blocks, saved = refs[2 * i], refs[2 * i + 1]
        total = blocks.shape[0] * half
        left.append(blocks[:, at : at + half, :].reshape(total, blocks.shape[2]))
        right.append(saved[first : first + total, :])
    left = jnp.concatenate(left, axis=0)
    right = jnp.concatenate(right, axis=0)
    if kind == "in":
        out[...] = dot(left, right, FIRST).astype(BF16)
    else:
        out[...] = dot(right, left, FIRST).astype(BF16)


def router_kernel(tokens, cotangent, rows, dispatch_in, combine_in, term, grad_logits_out):
    slots = grad_logits_out.shape[1]
    wide = 2 * slots
    dispatch, combine = dispatch_in[...], combine_in[...]
    inputs = input_columns(dispatch.shape)
    grad_combine = jnp.where(inputs, dot(cotangent[...], rows[...], WIDTH), 0.0)
    grad_dispatch = dot(tokens[...], rows[...], WIDTH)
    logit_combine = combine * (
        grad_combine - jnp.sum(combine * grad_combine, axis=1, keepdims=True)
    )
    logit_dispatch = dispatch * (
        grad_dispatch - jnp.sum(dispatch * grad_dispatch, axis=0, keepdims=True)
    )
    both = logit_combine + pltpu.roll(logit_dispatch, wide - 4, 1)
    both = jnp.where(inputs, both, 0.0).astype(BF16)
    grad_logits = dot(both, spread(slots, wide), WIDTH).astype(BF16)
    grad_logits_out[...] = grad_logits
    term[...] = dot(tokens[...], grad_logits, FIRST).astype(BF16)


def tokens_kernel(rows, router, dispatch_in, combine_in, grad_logits, mixed, grad_tokens):
    inputs = input_columns(dispatch_in.shape)
    combine_b = jnp.where(inputs, combine_in[...], 0.0).astype(BF16)
    dispatch_b = jnp.where(inputs, 0.0, dispatch_in[...]).astype(BF16)
    mixed[...] = dot(combine_b, rows[...], PLAIN).astype(BF16)
    through = dot(dispatch_b, rows[...], PLAIN) + dot(grad_logits[...], router[...], WIDTH)
    grad_tokens[...] = through.astype(BF16)


def shape(dims, dtype=BF16):
    return jax.ShapeDtypeStruct(dims, dtype)


def swap(value, axis):
    return lax.all_to_all(value, axis, split_axis=0, concat_axis=0, tiled=True)


def sum_router(term):
    slots = term.shape[1]
    n_plane = lax.axis_size(PLANE)
    n_z = lax.axis_size("z")
    share = swap(term.reshape(n_plane, term.shape[0] // n_plane, slots), PLANE)
    share = jnp.sum(share.astype(F32), axis=0).astype(BF16)
    share = swap(jnp.broadcast_to(share[None], (n_z,) + share.shape), "z")
    share = jnp.sum(share.astype(F32), axis=0).astype(BF16)
    full = swap(jnp.broadcast_to(share[None], (n_plane,) + share.shape), PLANE)
    return full.reshape(term.shape).astype(F32)


def per_device(tokens, router, expert_in, expert_out, cotangent):
    n_expert = lax.axis_size(EXPERT)
    count, width = tokens.shape
    slots = router.shape[1]
    wide = 2 * slots
    hidden_units = expert_in.shape[2]
    order = np.zeros((wide, wide), np.float32)
    order[np.arange(wide), row_order()] = 1.0
    order = jnp.asarray(order, BF16)

    rows, dispatch, combine = call(
        prologue_kernel,
        (shape((wide, width)), shape((count, wide), F32), shape((count, wide), F32)),
        (tokens, router, cotangent),
        6 * count * wide * width,
        "prologue",
    )
    rows = swap(rows.reshape(n_expert, 8, width), EXPERT).reshape(wide, width)
    parts = call(
        sort_kernel,
        tuple(shape((n, width)) for n in ROWS),
        (order, rows),
        2 * wide * wide * width,
        "sort",
    )

    near = [part[None] for part in parts]
    far = None
    for step in range(3):
        far = [
            lax.ppermute(near[p], DP, neighbour(ORDERS[p][step])) for p in range(len(PARTS))
        ]
        if step < 2:
            near = [jnp.concatenate([a, b], axis=0) for a, b in zip(near, far, strict=True)]

    def experts(p, blocks):
        n = blocks.shape[0]
        kept = shape((n * ROWS[p] // 2, hidden_units))
        return call(
            functools.partial(expert_kernel, PARTS[p]),
            (shape(blocks.shape), kept, kept),
            (blocks, expert_in, expert_out),
            4 * n * ROWS[p] * width * hidden_units,
            f"experts{p}",
        )

    near_done = [experts(p, near[p]) for p in range(len(PARTS))]
    far_done = [experts(p, far[p]) for p in range(len(PARTS))]

    sums = [done[0] for done in near_done]
    leaving = [done[0] for done in far_done]
    for step in (2, 1, 0):
        arrived = [
            lax.ppermute(leaving[p], DP, neighbour(ORDERS[p][step])) for p in range(len(PARTS))
        ]
        if step > 0:
            sums = [
                (a.astype(F32) + b.astype(F32)).astype(BF16)
                for a, b in zip(sums, arrived, strict=True)
            ]
            half = sums[0].shape[0] // 2
            leaving = [s[half:] for s in sums]
            sums = [s[:half] for s in sums]

    def weights(expert, kind):
        sections, args = [], []
        for p, part in enumerate(PARTS):
            for blocks, done in ((near[p], near_done[p]), (far[p], far_done[p])):
                at = saved = 0
                for owner, _, images in part:
                    half = 2 * images
                    if owner == expert:
                        sections.append((at + (0 if kind == "in" else half), half, saved))
                        args += [blocks, done[2 if kind == "in" else 1]]
                    at += 2 * half
                    saved += blocks.shape[0] * half
        dims = (width, hidden_units) if kind == "in" else (hidden_units, width)
        return call(
            functools.partial(weight_kernel, tuple(sections), kind),
            shape(dims),
            tuple(args),
            2 * 512 * width * hidden_units,
            f"weights_{kind}{expert}",
        )

    grad_in = jnp.stack([weights(0, "in"), weights(1, "in")])
    grad_out = jnp.stack([weights(0, "out"), weights(1, "out")])

    back = call(
        unsort_kernel,
        shape((wide, width)),
        (order, *(s[0] for s in sums), *(a[0] for a in arrived)),
        2 * wide * wide * width,
        "unsort",
    )
    back = swap(back.reshape(n_expert, 8, width), EXPERT).reshape(wide, width)
    term, grad_logits = call(
        router_kernel,
        (shape((width, slots)), shape((count, slots))),
        (tokens, cotangent, back, dispatch, combine),
        6 * count * wide * width,
        "router_gradient",
    )
    mixed, grad_tokens = call(
        tokens_kernel,
        (shape((count, width)), shape((count, width))),
        (back, router, dispatch, combine, grad_logits),
        5 * count * wide * width,
        "token_outputs",
    )
    return (mixed, grad_tokens, sum_router(term), grad_in, grad_out)


def solution(mesh):
    grid = Mesh(mesh.devices.reshape(2, 4, 8, 2, 2), ALL)
    in_specs = (
        P(ALL, None),
        P(),
        P(EXPERT, None, DP),
        P(EXPERT, DP, None),
        P(ALL, None),
    )
    out_specs = (
        P(ALL, None),
        P(ALL, None),
        P(),
        P(EXPERT, None, DP),
        P(EXPERT, DP, None),
    )
    return jax.shard_map(
        per_device, mesh=grid, in_specs=in_specs, out_specs=out_specs, check_vma=False
    )
```

```python
import functools
import math

import jax
import jax.numpy as jnp
from jax import lax
from jax.experimental import pallas as pl
from jax.experimental.pallas import tpu as pltpu
from jax.sharding import Mesh
from jax.sharding import PartitionSpec as P

F32 = jnp.float32
BF16 = jnp.bfloat16
ALL = ("xl", "yh", "yl", "z", "xh", "c")
DP = ("xl", "yh", "yl")
EXPERT = ("z", "xh", "c")
PLANE = ("xl", "yh", "yl", "xh", "c")

SECTION = 32
PART = 2 * SECTION
HALF = 2 * PART


def neighbour(dim):
    pairs = []
    for i in range(8):
        x, y = divmod(i, 4)
        if dim == "x":
            x = 1 - x
        elif dim == "y1":
            y = y ^ 1
        else:
            y = 3 - y
        pairs.append((i, x * 4 + y))
    return pairs


def call(kernel, out_shape, args, flops, name, scratch=(), memory=pltpu.VMEM, aliases=None):
    shapes = out_shape if isinstance(out_shape, tuple) else (out_shape,)
    moved = sum(math.prod(a.shape) * a.dtype.itemsize for a in tuple(args) + shapes)
    vmem = pl.BlockSpec(memory_space=memory)
    smem = pl.BlockSpec(memory_space=pltpu.SMEM)
    return pl.pallas_call(
        kernel,
        out_shape=out_shape,
        in_specs=[smem if a.dtype == jnp.int32 else vmem for a in args],
        out_specs=(vmem,) * len(shapes) if isinstance(out_shape, tuple) else vmem,
        compiler_params=pltpu.CompilerParams(vmem_limit_bytes=24 * 1024 * 1024),
        scratch_shapes=scratch,
        input_output_aliases=aliases or {},
        cost_estimate=pl.CostEstimate(flops=flops, bytes_accessed=moved, transcendentals=0),
        name=name,
    )(*args)


def dot(a, b, over):
    return lax.dot_general(a, b, (over, ((), ())), preferred_element_type=F32)


PLAIN = ((1,), (0,))
WIDTH = ((1,), (1,))
FIRST = ((0,), (0,))


def spread(slots, wide):
    row = lax.broadcasted_iota(jnp.int32, (slots, wide), 0)
    col = lax.broadcasted_iota(jnp.int32, (slots, wide), 1)
    return (row == 4 * (col // 8) + col % 4).astype(BF16)


def input_columns(shape):
    return lax.broadcasted_iota(jnp.int32, shape, 1) % 8 < 4


LANES = 128


def piece_copies(weights, at_expert, targets, sems, outward):
    copies = []
    target, at = targets[0], 0
    for matrix in weights:
        _, rows, columns = matrix.shape
        for lane in range(0, columns, LANES):
            if at == target.shape[0]:
                target, at = targets[1], 0
            ends = (matrix.at[at_expert, :, pl.ds(lane, LANES)], target.at[pl.ds(at, rows), :])
            source, place = ends if outward else ends[::-1]
            copies.append(pltpu.make_async_copy(source, place, sems.at[len(copies)]))
            at += rows
    for copy in copies:
        copy.start()
    for copy in copies:
        copy.wait()


def pack_kernel(side, expert_in, expert_out, first, second, sems):
    piece_copies((expert_in, expert_out), 1 - side[0], (first, second), sems, True)


def merge_kernel(side, first, second, kept_in, kept_out, grad_in, grad_out, sems):
    piece_copies((grad_in, grad_out), 1 - side[0], (first, second), sems, False)


def unpacked(first, second, width, hidden_units):
    held = first[...]
    cut = width * (hidden_units // LANES)
    w_in = [held[i : i + width] for i in range(0, cut, width)]
    w_out = [held[i : i + hidden_units] for i in range(cut, held.shape[0], hidden_units)]
    held = second[...]
    w_out += [held[i : i + hidden_units] for i in range(0, held.shape[0], hidden_units)]
    return jnp.concatenate(w_in, axis=1), jnp.concatenate(w_out, axis=1)


def prologue_kernel(tokens, router, cotangent, rows, dispatch_out, combine_out):
    slots = router.shape[1]
    wide = 2 * slots
    router_wide = dot(router[...], spread(slots, wide), PLAIN).astype(BF16)
    logits = dot(tokens[...], router_wide, PLAIN)
    down = jnp.exp(logits - jnp.max(logits, axis=0, keepdims=True))
    dispatch = down / jnp.sum(down, axis=0, keepdims=True)
    across = jnp.exp(logits - jnp.max(logits, axis=1, keepdims=True))
    combine = across / (0.5 * jnp.sum(across, axis=1, keepdims=True))
    inputs = input_columns(logits.shape)
    dispatch_b = jnp.where(inputs, dispatch, 0.0).astype(BF16)
    combine_b = jnp.where(inputs, 0.0, combine).astype(BF16)
    total = dot(dispatch_b, tokens[...], FIRST) + dot(combine_b, cotangent[...], FIRST)
    rows[...] = total.astype(BF16)
    dispatch_out[...] = dispatch
    combine_out[...] = combine


def sorting(side, wide):
    q = lax.broadcasted_iota(jnp.int32, (wide, wide), 0)
    r = lax.broadcasted_iota(jnp.int32, (wide, wide), 1)
    expert = (side + q // HALF) % 2
    image = 16 * ((q // PART) % 2) + (q % SECTION) // 2
    kind = (q // SECTION) % 2
    return (r == 8 * image + 4 * kind + 2 * expert + q % 2).astype(BF16)


def sort_kernel(side, rows, keep_a, keep_b, give):
    moved = dot(sorting(side[0], rows.shape[0]), rows[...], PLAIN).astype(BF16)
    keep_a[...] = moved[:PART]
    keep_b[...] = moved[PART:HALF]
    give[...] = moved[HALF:]


def add(a, b):
    return (a.astype(F32) + b.astype(F32)).astype(BF16)


def unsort_kernel(side, a, arrived_a, b, arrived_b, other, out):
    kept = [add(a[...], arrived_a[...]), add(b[...], arrived_b[...]), other[...]]
    rows = jnp.concatenate(kept, axis=0)
    out[...] = dot(sorting(side[0], rows.shape[0]), rows, FIRST).astype(BF16)


def gelu_parts(v):
    cdf = 0.5 * (1.0 + lax.erf(v * math.sqrt(0.5)))
    slope = cdf + v * (jnp.exp(-0.5 * v * v) * (1.0 / math.sqrt(2.0 * math.pi)))
    return v * cdf, slope


def rows_of(blocks, kind):
    first = kind * SECTION
    return jnp.concatenate(
        [
            b[:, first : first + SECTION, :].reshape(b.shape[0] * SECTION, b.shape[2])
            for b in blocks
        ],
        axis=0,
    )


def put_rows(blocks, kind, value):
    at = 0
    first = kind * SECTION
    for b in blocks:
        count = b.shape[0] * SECTION
        part = value[at : at + count].reshape(b.shape[0], SECTION, b.shape[2])
        b[:, first : first + SECTION, :] = part
        at += count


def expert_kernel(side, *refs):
    blocks, (in_all, out_all, first, second) = refs[:4], refs[4:8]
    results, act_out, hid_out = refs[8:12], refs[12], refs[13]
    in_more, out_more = unpacked(first, second, in_all.shape[1], in_all.shape[2])
    kept = side[0]
    rows, grads = rows_of(blocks, 0), rows_of(blocks, 1)
    slot_part = grad_part = 0.0
    for group in range(2):
        w_in = in_all[kept] if group == 0 else in_more
        w_out = out_all[kept] if group == 0 else out_more
        value, slope = gelu_parts(dot(rows, w_in, PLAIN))
        activated = value.astype(BF16)
        grad_hidden = (slope * dot(grads, w_out, WIDTH)).astype(BF16)
        act_out[group] = activated
        hid_out[group] = grad_hidden
        slot_part = slot_part + dot(activated, w_out, PLAIN)
        grad_part = grad_part + dot(grad_hidden, w_in, WIDTH)
    put_rows(results, 0, slot_part.astype(BF16))
    put_rows(results, 1, grad_part.astype(BF16))


def weight_gradients(group, refs):
    blocks, (act_0, act_1, hid_0, hid_1) = refs[:8], refs[8:12]
    rows, grads = rows_of(blocks, 0), rows_of(blocks, 1)
    hidden = jnp.concatenate([hid_0[group], hid_1[group]], axis=0)
    activated = jnp.concatenate([act_0[group], act_1[group]], axis=0)
    grad_in = dot(rows, hidden, FIRST).astype(BF16)
    return grad_in, dot(activated, grads, FIRST).astype(BF16)


def kept_weight_kernel(side, *refs):
    grad_in, grad_out = refs[12:]
    grad_in[side[0]], grad_out[side[0]] = weight_gradients(0, refs)


def given_weight_kernel(*refs):
    targets = refs[12:]
    target, at = targets[0], 0
    for value in weight_gradients(1, refs):
        rows, columns = value.shape
        for lane in range(0, columns, LANES):
            if at == target.shape[0]:
                target, at = targets[1], 0
            target[at : at + rows, :] = value[:, lane : lane + LANES]
            at += rows


def share_kernel(partials, out):
    total = jnp.sum(partials[...].astype(F32), axis=0).astype(BF16)
    for i in range(out.shape[0]):
        out[i] = total


def router_kernel(tokens, cotangent, rows, dispatch_in, combine_in, term, grad_logits_out):
    slots = grad_logits_out.shape[1]
    wide = 2 * slots
    dispatch, combine = dispatch_in[...], combine_in[...]
    inputs = input_columns(dispatch.shape)
    grad_combine = jnp.where(inputs, dot(cotangent[...], rows[...], WIDTH), 0.0)
    grad_dispatch = dot(tokens[...], rows[...], WIDTH)
    logit_combine = combine * (
        grad_combine - jnp.sum(combine * grad_combine, axis=1, keepdims=True)
    )
    logit_dispatch = dispatch * (
        grad_dispatch - jnp.sum(dispatch * grad_dispatch, axis=0, keepdims=True)
    )
    both = logit_combine + pltpu.roll(logit_dispatch, wide - 4, 1)
    both = jnp.where(inputs, both, 0.0).astype(BF16)
    grad_logits = dot(both, spread(slots, wide), WIDTH).astype(BF16)
    grad_logits_out[...] = grad_logits
    term[...] = dot(tokens[...], grad_logits, FIRST).astype(BF16)


def tokens_kernel(rows, router, dispatch_in, combine_in, grad_logits, mixed, grad_tokens):
    inputs = input_columns(dispatch_in.shape)
    combine_b = jnp.where(inputs, combine_in[...], 0.0).astype(BF16)
    dispatch_b = jnp.where(inputs, 0.0, dispatch_in[...]).astype(BF16)
    mixed[...] = dot(combine_b, rows[...], PLAIN).astype(BF16)
    through = dot(dispatch_b, rows[...], PLAIN) + dot(grad_logits[...], router[...], WIDTH)
    grad_tokens[...] = through.astype(BF16)


def shape(dims, dtype=BF16):
    return jax.ShapeDtypeStruct(dims, dtype)


def swap(value, axis):
    return lax.all_to_all(value, axis, split_axis=0, concat_axis=0, tiled=True)


def sum_router(term):
    slots = term.shape[1]
    n_plane = lax.axis_size(PLANE)
    n_z = lax.axis_size("z")
    block = (term.shape[0] // n_plane, slots)
    share = swap(term.reshape((n_plane,) + block), PLANE)
    share = call(share_kernel, shape((n_z,) + block), (share,), 0, "share_plane")
    share = swap(share, "z")
    share = call(share_kernel, shape((n_plane,) + block), (share,), 0, "share_z")
    return swap(share, PLANE).reshape(term.shape).astype(F32)


def per_device(tokens, router, expert_in, expert_out, cotangent):
    n_expert = lax.axis_size(EXPERT)
    count, width = tokens.shape
    slots = router.shape[1]
    wide = 2 * slots
    hidden_units = expert_in.shape[2]
    tied = lax.optimization_barrier
    row, pair = lax.axis_index("yl"), lax.axis_index("yh")
    place = (row + pair) % 2
    side = place.astype(jnp.int32).reshape(1)

    def exchange(value, dim):
        return lax.ppermute(value, DP, neighbour(dim))

    pieces = hidden_units // LANES + width // LANES
    pieces = hidden_units // LANES + width // LANES
    whole = 2 * width * hidden_units // LANES

    def cut(in_pieces, out_pieces):
        first = in_pieces * width + out_pieces * hidden_units
        return shape((first, LANES)), shape((whole - first, LANES))

    copy_sems = (pltpu.SemaphoreType.DMA((pieces,)),)
    packed, packed_late = call(
        pack_kernel,
        cut(3, 3),
        (side, expert_in, expert_out),
        0,
        "pack",
        copy_sems,
        pl.ANY,
    )
    packed, router = tied((packed, router))
    more = exchange(packed, "y1")

    rows, dispatch, combine = call(
        prologue_kernel,
        (shape((wide, width)), shape((count, wide), F32), shape((count, wide), F32)),
        (tokens, router, cotangent),
        6 * count * wide * width,
        "prologue",
    )
    rows = swap(rows.reshape(n_expert, 8, width), EXPERT).reshape(wide, width)
    rows, more = tied((rows, more))
    keep_a, keep_b, give = call(
        sort_kernel,
        (shape((PART, width)), shape((PART, width)), shape((HALF, width))),
        (side, rows),
        2 * wide * wide * width,
        "sort",
    )

    def gather(a, b):
        a, b = a[None], b[None]
        near_a = jnp.concatenate([a, exchange(a, "x")], axis=0)
        near_b = jnp.concatenate([b, exchange(b, "y3")], axis=0)
        near_a, near_b = tied((near_a, near_b))
        return near_a, near_b, exchange(near_a, "y3"), exchange(near_b, "x")

    def experts(blocks, name):
        kept = shape((2, 4 * PART, hidden_units))
        done = call(
            expert_kernel,
            tuple(shape(b.shape) for b in blocks) + (kept, kept),
            (side, *blocks, expert_in, expert_out, more, more_late),
            16 * 4 * PART * width * hidden_units,
            name,
        )
        return done[:4], done[4], done[5]

    taken = exchange(give, "y1")
    packed_late, taken = tied((packed_late, taken))
    more_late = exchange(packed_late, "y1")
    own = gather(keep_a, keep_b)
    partner = gather(taken[:PART], taken[PART:])
    own_done, own_act, own_hid = experts(own, "experts_own")
    far_a, far_b, own_done = tied((partner[2], partner[3], own_done))
    partner = (partner[0], partner[1], far_a, far_b)
    partner_done, partner_act, partner_hid = experts(partner, "experts_partner")

    known = (*own, *partner, own_act, partner_act, own_hid, partner_hid)
    work = 4 * 8 * PART * width * hidden_units
    theirs = call(given_weight_kernel, cut(2, 0), known, work, "weights_given")
    mine = call(
        kept_weight_kernel,
        (shape(expert_in.shape), shape(expert_out.shape)),
        (side, *known),
        work,
        "weights_kept",
    )

    def scatter(done, also):
        near_a, near_b, far_a, far_b = done
        near_a = add(near_a, exchange(far_a, "y3"))
        near_b = add(near_b, exchange(far_b, "x"))
        near_a, near_b, also = tied((near_a, near_b, also))
        arrived_a, arrived_b = exchange(near_a[1], "x"), exchange(near_b[1], "y3")
        return (near_a[0], arrived_a, near_b[0], arrived_b), also

    received = exchange(theirs[0], "y1")
    partner_sum, mine = scatter(partner_done, mine)
    own_sum, _ = scatter(own_done, ())
    a, arrived_a, b, arrived_b = partner_sum
    ready = jnp.concatenate([add(a, arrived_a), add(b, arrived_b)], axis=0)
    ready, received = tied((ready, received))
    returned = exchange(ready, "y1")
    back = call(
        unsort_kernel,
        shape((wide, width)),
        (side, *own_sum, returned),
        2 * wide * wide * width,
        "unsort",
    )
    back, leaving = tied((back, theirs[1]))
    received_late = exchange(leaving, "y1")
    back = swap(back.reshape(n_expert, 8, width), EXPERT).reshape(wide, width)
    term, grad_logits = call(
        router_kernel,
        (shape((width, slots)), shape((count, slots))),
        (tokens, cotangent, back, dispatch, combine),
        6 * count * wide * width,
        "router_gradient",
    )
    mixed, grad_tokens = call(
        tokens_kernel,
        (shape((count, width)), shape((count, width))),
        (back, router, dispatch, combine, grad_logits),
        5 * count * wide * width,
        "token_outputs",
    )
    grad_router = sum_router(term)
    grad_in, grad_out = call(
        merge_kernel,
        (shape(expert_in.shape), shape(expert_out.shape)),
        (side, received, received_late, *mine),
        0,
        "merge",
        copy_sems,
        pl.ANY,
        {3: 0, 4: 1},
    )
    return (mixed, grad_tokens, grad_router, grad_in, grad_out)


def solution(mesh):
    grid = Mesh(mesh.devices.reshape(2, 2, 2, 8, 2, 2), ALL)
    in_specs = (
        P(ALL, None),
        P(),
        P(EXPERT, None, DP),
        P(EXPERT, DP, None),
        P(ALL, None),
    )
    out_specs = (
        P(ALL, None),
        P(ALL, None),
        P(),
        P(EXPERT, None, DP),
        P(EXPERT, DP, None),
    )
    return jax.shard_map(
        per_device, mesh=grid, in_specs=in_specs, out_specs=out_specs, check_vma=False
    )
```

```python
import functools
import math

import jax
import jax.numpy as jnp
from jax import lax
from jax.experimental import pallas as pl
from jax.experimental.pallas import tpu as pltpu
from jax.sharding import Mesh
from jax.sharding import PartitionSpec as P

F32 = jnp.float32
BF16 = jnp.bfloat16
ALL = ("xl", "yh", "yl", "z", "xh", "c")
DP = ("xl", "yh", "yl")
EXPERT = ("z", "xh", "c")
PLANE = ("xl", "yh", "yl", "xh")
CORES = [(0, 1), (1, 0)]

SECTION = 32
PART = 2 * SECTION
HALF = 2 * PART


def neighbour(dim):
    pairs = []
    for i in range(8):
        x, y = divmod(i, 4)
        if dim == "x":
            x = 1 - x
        elif dim == "y1":
            y = y ^ 1
        else:
            y = 3 - y
        pairs.append((i, x * 4 + y))
    return pairs


def call(kernel, out_shape, args, flops, name, scratch=(), memory=pltpu.VMEM, aliases=None):
    shapes = out_shape if isinstance(out_shape, tuple) else (out_shape,)
    moved = sum(math.prod(a.shape) * a.dtype.itemsize for a in tuple(args) + shapes)
    vmem = pl.BlockSpec(memory_space=memory)
    smem = pl.BlockSpec(memory_space=pltpu.SMEM)
    return pl.pallas_call(
        kernel,
        out_shape=out_shape,
        in_specs=[smem if a.dtype == jnp.int32 else vmem for a in args],
        out_specs=(vmem,) * len(shapes) if isinstance(out_shape, tuple) else vmem,
        compiler_params=pltpu.CompilerParams(vmem_limit_bytes=24 * 1024 * 1024),
        scratch_shapes=scratch,
        input_output_aliases=aliases or {},
        cost_estimate=pl.CostEstimate(flops=flops, bytes_accessed=moved, transcendentals=0),
        name=name,
    )(*args)


def dot(a, b, over):
    return lax.dot_general(a, b, (over, ((), ())), preferred_element_type=F32)


PLAIN = ((1,), (0,))
WIDTH = ((1,), (1,))
FIRST = ((0,), (0,))


def spread(slots, wide):
    row = lax.broadcasted_iota(jnp.int32, (slots, wide), 0)
    col = lax.broadcasted_iota(jnp.int32, (slots, wide), 1)
    return (row == 4 * (col // 8) + col % 4).astype(BF16)


def input_columns(shape):
    return lax.broadcasted_iota(jnp.int32, shape, 1) % 8 < 4


LANES = 128


def piece_copies(weights, at_expert, targets, sems, outward):
    copies = []
    target, at = targets[0], 0
    for matrix in weights:
        _, rows, columns = matrix.shape
        for lane in range(0, columns, LANES):
            if at == target.shape[0]:
                target, at = targets[1], 0
            ends = (matrix.at[at_expert, :, pl.ds(lane, LANES)], target.at[pl.ds(at, rows), :])
            source, place = ends if outward else ends[::-1]
            copies.append(pltpu.make_async_copy(source, place, sems.at[len(copies)]))
            at += rows
    for copy in copies:
        copy.start()
    for copy in copies:
        copy.wait()


def pack_kernel(side, expert_in, expert_out, first, second, sems):
    piece_copies((expert_in, expert_out), 1 - side[0], (first, second), sems, True)


def merge_kernel(side, first, second, kept_in, kept_out, grad_in, grad_out, sems):
    piece_copies((grad_in, grad_out), 1 - side[0], (first, second), sems, False)


def unpacked(first, second, width, hidden_units):
    held = first[...]
    cut = width * (hidden_units // LANES)
    w_in = [held[i : i + width] for i in range(0, cut, width)]
    w_out = [held[i : i + hidden_units] for i in range(cut, held.shape[0], hidden_units)]
    held = second[...]
    w_out += [held[i : i + hidden_units] for i in range(0, held.shape[0], hidden_units)]
    return jnp.concatenate(w_in, axis=1), jnp.concatenate(w_out, axis=1)


def prologue_kernel(tokens, router, cotangent, rows, dispatch_out, combine_out):
    slots = router.shape[1]
    wide = 2 * slots
    router_wide = dot(router[...], spread(slots, wide), PLAIN).astype(BF16)
    logits = dot(tokens[...], router_wide, PLAIN)
    down = jnp.exp(logits - jnp.max(logits, axis=0, keepdims=True))
    dispatch = down / jnp.sum(down, axis=0, keepdims=True)
    across = jnp.exp(logits - jnp.max(logits, axis=1, keepdims=True))
    combine = across / (0.5 * jnp.sum(across, axis=1, keepdims=True))
    inputs = input_columns(logits.shape)
    dispatch_b = jnp.where(inputs, dispatch, 0.0).astype(BF16)
    combine_b = jnp.where(inputs, 0.0, combine).astype(BF16)
    total = dot(dispatch_b, tokens[...], FIRST) + dot(combine_b, cotangent[...], FIRST)
    rows[...] = total.astype(BF16)
    dispatch_out[...] = dispatch
    combine_out[...] = combine


def sorting(side, wide):
    q = lax.broadcasted_iota(jnp.int32, (wide, wide), 0)
    r = lax.broadcasted_iota(jnp.int32, (wide, wide), 1)
    expert = (side + q // HALF) % 2
    image = 16 * ((q // PART) % 2) + (q % SECTION) // 2
    kind = (q // SECTION) % 2
    return (r == 8 * image + 4 * kind + 2 * expert + q % 2).astype(BF16)


def sort_kernel(side, rows, keep_a, keep_b, give):
    moved = dot(sorting(side[0], rows.shape[0]), rows[...], PLAIN).astype(BF16)
    keep_a[...] = moved[:PART]
    keep_b[...] = moved[PART:HALF]
    give[...] = moved[HALF:]


def add(a, b):
    return (a.astype(F32) + b.astype(F32)).astype(BF16)


def unsort_kernel(side, a, arrived_a, b, arrived_b, other, out):
    kept = [add(a[...], arrived_a[...]), add(b[...], arrived_b[...]), other[...]]
    rows = jnp.concatenate(kept, axis=0)
    out[...] = dot(sorting(side[0], rows.shape[0]), rows, FIRST).astype(BF16)


def gelu_parts(v):
    cdf = 0.5 * (1.0 + lax.erf(v * math.sqrt(0.5)))
    slope = cdf + v * (jnp.exp(-0.5 * v * v) * (1.0 / math.sqrt(2.0 * math.pi)))
    return v * cdf, slope


def rows_of(blocks, kind):
    first = kind * SECTION
    return jnp.concatenate(
        [
            b[:, first : first + SECTION, :].reshape(b.shape[0] * SECTION, b.shape[2])
            for b in blocks
        ],
        axis=0,
    )


def put_rows(blocks, kind, value):
    at = 0
    first = kind * SECTION
    for b in blocks:
        count = b.shape[0] * SECTION
        part = value[at : at + count].reshape(b.shape[0], SECTION, b.shape[2])
        b[:, first : first + SECTION, :] = part
        at += count


def expert_kernel(side, *refs):
    blocks, (in_all, out_all, first, second) = refs[:4], refs[4:8]
    results, act_out, hid_out = refs[8:12], refs[12], refs[13]
    in_more, out_more = unpacked(first, second, in_all.shape[1], in_all.shape[2])
    kept = side[0]
    rows, grads = rows_of(blocks, 0), rows_of(blocks, 1)
    slot_part = grad_part = 0.0
    for group in range(2):
        w_in = in_all[kept] if group == 0 else in_more
        w_out = out_all[kept] if group == 0 else out_more
        value, slope = gelu_parts(dot(rows, w_in, PLAIN))
        activated = value.astype(BF16)
        grad_hidden = (slope * dot(grads, w_out, WIDTH)).astype(BF16)
        act_out[group] = activated
        hid_out[group] = grad_hidden
        slot_part = slot_part + dot(activated, w_out, PLAIN)
        grad_part = grad_part + dot(grad_hidden, w_in, WIDTH)
    put_rows(results, 0, slot_part.astype(BF16))
    put_rows(results, 1, grad_part.astype(BF16))


def weight_gradients(group, refs):
    blocks, (act_0, act_1, hid_0, hid_1) = refs[:8], refs[8:12]
    rows, grads = rows_of(blocks, 0), rows_of(blocks, 1)
    hidden = jnp.concatenate([hid_0[group], hid_1[group]], axis=0)
    activated = jnp.concatenate([act_0[group], act_1[group]], axis=0)
    grad_in = dot(rows, hidden, FIRST).astype(BF16)
    return grad_in, dot(activated, grads, FIRST).astype(BF16)


def kept_weight_kernel(side, *refs):
    grad_in, grad_out = refs[12:]
    grad_in[side[0]], grad_out[side[0]] = weight_gradients(0, refs)


def given_weight_kernel(*refs):
    targets = refs[12:]
    target, at = targets[0], 0
    for value in weight_gradients(1, refs):
        rows, columns = value.shape
        for lane in range(0, columns, LANES):
            if at == target.shape[0]:
                target, at = targets[1], 0
            target[at : at + rows, :] = value[:, lane : lane + LANES]
            at += rows


def share_kernel(partials, out):
    total = jnp.sum(partials[...].astype(F32), axis=0).astype(BF16)
    for i in range(out.shape[0]):
        out[i] = total


def by_core(core, first, second):
    return jnp.where(core == 0, first, second), jnp.where(core == 0, second, first)


def router_kernel(
    core, tokens, cotangent, rows, dispatch_in, combine_in, keep, give, grad_logits_out
):
    slots = grad_logits_out.shape[1]
    wide = 2 * slots
    dispatch, combine = dispatch_in[...], combine_in[...]
    inputs = input_columns(dispatch.shape)
    grad_combine = jnp.where(inputs, dot(cotangent[...], rows[...], WIDTH), 0.0)
    grad_dispatch = dot(tokens[...], rows[...], WIDTH)
    logit_combine = combine * (
        grad_combine - jnp.sum(combine * grad_combine, axis=1, keepdims=True)
    )
    logit_dispatch = dispatch * (
        grad_dispatch - jnp.sum(dispatch * grad_dispatch, axis=0, keepdims=True)
    )
    both = logit_combine + pltpu.roll(logit_dispatch, wide - 4, 1)
    both = jnp.where(inputs, both, 0.0).astype(BF16)
    grad_logits = dot(both, spread(slots, wide), WIDTH).astype(BF16)
    grad_logits_out[...] = grad_logits
    term = dot(tokens[...], grad_logits, FIRST)
    kept, given = by_core(core[0], term[: keep.shape[0]], term[keep.shape[0] :])
    keep[...] = kept.astype(BF16)
    give[...] = given.astype(BF16)


def tokens_kernel(rows, router, dispatch_in, combine_in, grad_logits, mixed, grad_tokens):
    inputs = input_columns(dispatch_in.shape)
    combine_b = jnp.where(inputs, combine_in[...], 0.0).astype(BF16)
    dispatch_b = jnp.where(inputs, 0.0, dispatch_in[...]).astype(BF16)
    mixed[...] = dot(combine_b, rows[...], PLAIN).astype(BF16)
    through = dot(dispatch_b, rows[...], PLAIN) + dot(grad_logits[...], router[...], WIDTH)
    grad_tokens[...] = through.astype(BF16)


def pair_kernel(keep, received, out):
    out[...] = add(keep[...], received[...])


def widen_kernel(core, kept, received, out):
    half = out.shape[0] // 2
    kept = kept[...].astype(F32).reshape(half, out.shape[1])
    received = received[...].astype(F32).reshape(half, out.shape[1])
    out[:half, :], out[half:, :] = by_core(core[0], kept, received)


def shape(dims, dtype=BF16):
    return jax.ShapeDtypeStruct(dims, dtype)


def swap(value, axis):
    return lax.all_to_all(value, axis, split_axis=0, concat_axis=0, tiled=True)


def sum_router(keep, give, core, others):
    half, slots = keep.shape
    n_plane = lax.axis_size(PLANE)
    n_z = lax.axis_size("z")
    block = (half // n_plane, slots)
    received = lax.ppermute(give, "c", CORES)
    share = call(pair_kernel, shape(keep.shape), (keep, received), 0, "pair")
    share = swap(share.reshape((n_plane,) + block), PLANE)
    share = call(share_kernel, shape((n_z,) + block), (share,), 0, "share_plane")
    share = swap(share, "z")
    share = call(share_kernel, shape((n_plane,) + block), (share,), 0, "share_z")
    share, others = lax.optimization_barrier((swap(share, PLANE), others))
    received = lax.ppermute(share, "c", CORES)
    full = shape((2 * half, slots), F32)
    return call(widen_kernel, full, (core, share, received), 0, "widen"), others


def per_device(tokens, router, expert_in, expert_out, cotangent):
    n_expert = lax.axis_size(EXPERT)
    count, width = tokens.shape
    slots = router.shape[1]
    wide = 2 * slots
    hidden_units = expert_in.shape[2]
    tied = lax.optimization_barrier
    row, pair = lax.axis_index("yl"), lax.axis_index("yh")
    place = (row + pair) % 2
    side = place.astype(jnp.int32).reshape(1)
    core = lax.axis_index("c").astype(jnp.int32).reshape(1)

    def exchange(value, dim):
        return lax.ppermute(value, DP, neighbour(dim))

    pieces = hidden_units // LANES + width // LANES
    pieces = hidden_units // LANES + width // LANES
    whole = 2 * width * hidden_units // LANES

    def cut(in_pieces, out_pieces):
        first = in_pieces * width + out_pieces * hidden_units
        return shape((first, LANES)), shape((whole - first, LANES))

    copy_sems = (pltpu.SemaphoreType.DMA((pieces,)),)
    packed, packed_late = call(
        pack_kernel,
        cut(3, 3),
        (side, expert_in, expert_out),
        0,
        "pack",
        copy_sems,
        pl.ANY,
    )
    packed, router = tied((packed, router))
    more = exchange(packed, "y1")

    rows, dispatch, combine = call(
        prologue_kernel,
        (shape((wide, width)), shape((count, wide), F32), shape((count, wide), F32)),
        (tokens, router, cotangent),
        6 * count * wide * width,
        "prologue",
    )
    rows = swap(rows.reshape(n_expert, 8, width), EXPERT).reshape(wide, width)
    rows, more = tied((rows, more))
    keep_a, keep_b, give = call(
        sort_kernel,
        (shape((PART, width)), shape((PART, width)), shape((HALF, width))),
        (side, rows),
        2 * wide * wide * width,
        "sort",
    )

    def first_step(a, b):
        a, b = a[None], b[None]
        near_a = jnp.concatenate([a, exchange(a, "x")], axis=0)
        near_b = jnp.concatenate([b, exchange(b, "y3")], axis=0)
        return tied((near_a, near_b))

    def second_step(a, b):
        return a, b, exchange(a, "y3"), exchange(b, "x")

    def experts(blocks, name):
        kept = shape((2, 4 * PART, hidden_units))
        done = call(
            expert_kernel,
            tuple(shape(b.shape) for b in blocks) + (kept, kept),
            (side, *blocks, expert_in, expert_out, more, more_late),
            16 * 4 * PART * width * hidden_units,
            name,
        )
        return done[:4], done[4], done[5]

    taken = exchange(give, "y1")
    packed_late, taken = tied((packed_late, taken))
    more_late = exchange(packed_late, "y1")
    partner = first_step(taken[:PART], taken[PART:])
    own = first_step(keep_a, keep_b)
    partner, own = tied((partner, own))
    partner, own = second_step(*partner), second_step(*own)
    partner_done, partner_act, partner_hid = experts(partner, "experts_partner")
    far_a, far_b, partner_done = tied((own[2], own[3], partner_done))
    own = (own[0], own[1], far_a, far_b)
    own_done, own_act, own_hid = experts(own, "experts_own")

    known = (*own, *partner, own_act, partner_act, own_hid, partner_hid)
    work = 4 * 8 * PART * width * hidden_units
    theirs = call(given_weight_kernel, cut(2, 0), known, work, "weights_given")
    mine = call(
        kept_weight_kernel,
        (shape(expert_in.shape), shape(expert_out.shape)),
        (side, *known),
        work,
        "weights_kept",
    )

    def first_sum(near_a, near_b, far_a, far_b):
        return add(near_a, exchange(far_a, "y3")), add(near_b, exchange(far_b, "x"))

    def second_sum(near_a, near_b, also):
        near_a, near_b, also = tied((near_a, near_b, also))
        arrived_a, arrived_b = exchange(near_a[1], "x"), exchange(near_b[1], "y3")
        return (near_a[0], arrived_a, near_b[0], arrived_b), also

    received = exchange(theirs[0], "y1")
    partner_sum = first_sum(*partner_done)
    partner_sum, own_done = tied((partner_sum, own_done))
    partner_sum, _ = second_sum(*partner_sum, ())
    own_sum, mine = second_sum(*first_sum(*own_done), mine)
    a, arrived_a, b, arrived_b = partner_sum
    ready = jnp.concatenate([add(a, arrived_a), add(b, arrived_b)], axis=0)
    ready, received = tied((ready, received))
    returned = exchange(ready, "y1")
    back = call(
        unsort_kernel,
        shape((wide, width)),
        (side, *own_sum, returned),
        2 * wide * wide * width,
        "unsort",
    )
    back, leaving = tied((back, theirs[1]))
    received_late = exchange(leaving, "y1")
    back = swap(back.reshape(n_expert, 8, width), EXPERT).reshape(wide, width)
    keep, give, grad_logits = call(
        router_kernel,
        (shape((width // 2, slots)), shape((width // 2, slots)), shape((count, slots))),
        (core, tokens, cotangent, back, dispatch, combine),
        6 * count * wide * width,
        "router_gradient",
    )
    mixed, grad_tokens = call(
        tokens_kernel,
        (shape((count, width)), shape((count, width))),
        (back, router, dispatch, combine, grad_logits),
        5 * count * wide * width,
        "token_outputs",
    )
    grad_in, grad_out = call(
        merge_kernel,
        (shape(expert_in.shape), shape(expert_out.shape)),
        (side, received, received_late, *mine),
        0,
        "merge",
        copy_sems,
        pl.ANY,
        {3: 0, 4: 1},
    )
    grad_router, others = sum_router(
        keep, give, core, (mixed, grad_tokens, grad_in, grad_out)
    )
    mixed, grad_tokens, grad_in, grad_out = others
    return (mixed, grad_tokens, grad_router, grad_in, grad_out)


def solution(mesh):
    grid = Mesh(mesh.devices.reshape(2, 2, 2, 8, 2, 2), ALL)
    in_specs = (
        P(ALL, None),
        P(),
        P(EXPERT, None, DP),
        P(EXPERT, DP, None),
        P(ALL, None),
    )
    out_specs = (
        P(ALL, None),
        P(ALL, None),
        P(),
        P(EXPERT, None, DP),
        P(EXPERT, DP, None),
    )
    return jax.shard_map(
        per_device, mesh=grid, in_specs=in_specs, out_specs=out_specs, check_vma=False
    )
```

```python
import functools
import math

import jax
import jax.numpy as jnp
from jax import lax
from jax.experimental import pallas as pl
from jax.experimental.pallas import tpu as pltpu
from jax.sharding import Mesh
from jax.sharding import PartitionSpec as P

F32 = jnp.float32
BF16 = jnp.bfloat16
ALL = ("xl", "yh", "yl", "z", "xh", "c")
DP = ("xl", "yh", "yl")
EXPERT = ("z", "xh", "c")
PLANE = ("xl", "yh", "yl", "xh")
CORES = [(0, 1), (1, 0)]

SECTION = 32
PART = 2 * SECTION
HALF = 2 * PART


def neighbour(dim):
    pairs = []
    for i in range(8):
        x, y = divmod(i, 4)
        if dim == "x":
            x = 1 - x
        elif dim == "y1":
            y = y ^ 1
        else:
            y = 3 - y
        pairs.append((i, x * 4 + y))
    return pairs


def call(kernel, out_shape, args, flops, name, scratch=(), memory=pltpu.VMEM, aliases=None):
    shapes = out_shape if isinstance(out_shape, tuple) else (out_shape,)
    moved = sum(math.prod(a.shape) * a.dtype.itemsize for a in tuple(args) + shapes)
    vmem = pl.BlockSpec(memory_space=memory)
    smem = pl.BlockSpec(memory_space=pltpu.SMEM)
    return pl.pallas_call(
        kernel,
        out_shape=out_shape,
        in_specs=[smem if a.dtype == jnp.int32 else vmem for a in args],
        out_specs=(vmem,) * len(shapes) if isinstance(out_shape, tuple) else vmem,
        compiler_params=pltpu.CompilerParams(vmem_limit_bytes=24 * 1024 * 1024),
        scratch_shapes=scratch,
        input_output_aliases=aliases or {},
        cost_estimate=pl.CostEstimate(flops=flops, bytes_accessed=moved, transcendentals=0),
        name=name,
    )(*args)


def dot(a, b, over):
    return lax.dot_general(a, b, (over, ((), ())), preferred_element_type=F32)


PLAIN = ((1,), (0,))
WIDTH = ((1,), (1,))
FIRST = ((0,), (0,))


def spread(slots, wide):
    row = lax.broadcasted_iota(jnp.int32, (slots, wide), 0)
    col = lax.broadcasted_iota(jnp.int32, (slots, wide), 1)
    return (row == 4 * (col // 8) + col % 4).astype(BF16)


def input_columns(shape):
    return lax.broadcasted_iota(jnp.int32, shape, 1) % 8 < 4


LANES = 128


def piece_copies(weights, at_expert, targets, sems, outward):
    copies = []
    target, at = targets[0], 0
    for matrix in weights:
        _, rows, columns = matrix.shape
        for lane in range(0, columns, LANES):
            if at == target.shape[0]:
                target, at = targets[1], 0
            ends = (matrix.at[at_expert, :, pl.ds(lane, LANES)], target.at[pl.ds(at, rows), :])
            source, place = ends if outward else ends[::-1]
            copies.append(pltpu.make_async_copy(source, place, sems.at[len(copies)]))
            at += rows
    for copy in copies:
        copy.start()
    for copy in copies:
        copy.wait()


def pack_kernel(side, expert_in, expert_out, first, second, sems):
    piece_copies((expert_in, expert_out), 1 - side[0], (first, second), sems, True)


def merge_kernel(side, first, second, kept_in, kept_out, grad_in, grad_out, sems):
    piece_copies((grad_in, grad_out), 1 - side[0], (first, second), sems, False)


def unpacked(first, second, width, hidden_units):
    held = first[...]
    cut = width * (hidden_units // LANES)
    w_in = [held[i : i + width] for i in range(0, cut, width)]
    w_out = [held[i : i + hidden_units] for i in range(cut, held.shape[0], hidden_units)]
    held = second[...]
    w_out += [held[i : i + hidden_units] for i in range(0, held.shape[0], hidden_units)]
    return jnp.concatenate(w_in, axis=1), jnp.concatenate(w_out, axis=1)


def prologue_kernel(tokens, router, cotangent, rows, dispatch_out, combine_out):
    slots = router.shape[1]
    wide = 2 * slots
    router_wide = dot(router[...], spread(slots, wide), PLAIN).astype(BF16)
    logits = dot(tokens[...], router_wide, PLAIN)
    down = jnp.exp(logits - jnp.max(logits, axis=0, keepdims=True))
    dispatch = down / jnp.sum(down, axis=0, keepdims=True)
    across = jnp.exp(logits - jnp.max(logits, axis=1, keepdims=True))
    combine = across / (0.5 * jnp.sum(across, axis=1, keepdims=True))
    inputs = input_columns(logits.shape)
    dispatch_b = jnp.where(inputs, dispatch, 0.0).astype(BF16)
    combine_b = jnp.where(inputs, 0.0, combine).astype(BF16)
    total = dot(dispatch_b, tokens[...], FIRST) + dot(combine_b, cotangent[...], FIRST)
    rows[...] = total.astype(BF16)
    dispatch_out[...] = dispatch
    combine_out[...] = combine


def sorting(side, wide):
    q = lax.broadcasted_iota(jnp.int32, (wide, wide), 0)
    r = lax.broadcasted_iota(jnp.int32, (wide, wide), 1)
    expert = (side + q // HALF) % 2
    image = 16 * ((q // PART) % 2) + (q % SECTION) // 2
    kind = (q // SECTION) % 2
    return (r == 8 * image + 4 * kind + 2 * expert + q % 2).astype(BF16)


def sort_kernel(side, rows, keep_a, keep_b, give):
    moved = dot(sorting(side[0], rows.shape[0]), rows[...], PLAIN).astype(BF16)
    keep_a[...] = moved[:PART]
    keep_b[...] = moved[PART:HALF]
    give[...] = moved[HALF:]


def add(a, b):
    return (a.astype(F32) + b.astype(F32)).astype(BF16)


def unsort_kernel(side, a, arrived_a, b, arrived_b, other, out):
    kept = [add(a[...], arrived_a[...]), add(b[...], arrived_b[...]), other[...]]
    rows = jnp.concatenate(kept, axis=0)
    out[...] = dot(sorting(side[0], rows.shape[0]), rows, FIRST).astype(BF16)


def gelu_parts(v):
    cdf = 0.5 * (1.0 + lax.erf(v * math.sqrt(0.5)))
    slope = cdf + v * (jnp.exp(-0.5 * v * v) * (1.0 / math.sqrt(2.0 * math.pi)))
    return v * cdf, slope


def rows_of(blocks, kind):
    first = kind * SECTION
    return jnp.concatenate(
        [
            b[:, first : first + SECTION, :].reshape(b.shape[0] * SECTION, b.shape[2])
            for b in blocks
        ],
        axis=0,
    )


def put_rows(blocks, kind, value):
    at = 0
    first = kind * SECTION
    for b in blocks:
        count = b.shape[0] * SECTION
        part = value[at : at + count].reshape(b.shape[0], SECTION, b.shape[2])
        b[:, first : first + SECTION, :] = part
        at += count


def expert_kernel(side, *refs):
    blocks, (in_all, out_all, first, second) = refs[:4], refs[4:8]
    results, act_out, hid_out = refs[8:12], refs[12], refs[13]
    in_more, out_more = unpacked(first, second, in_all.shape[1], in_all.shape[2])
    kept = side[0]
    rows, grads = rows_of(blocks, 0), rows_of(blocks, 1)
    slot_part = grad_part = 0.0
    for group in range(2):
        w_in = in_all[kept] if group == 0 else in_more
        w_out = out_all[kept] if group == 0 else out_more
        value, slope = gelu_parts(dot(rows, w_in, PLAIN))
        activated = value.astype(BF16)
        grad_hidden = (slope * dot(grads, w_out, WIDTH)).astype(BF16)
        act_out[group] = activated
        hid_out[group] = grad_hidden
        slot_part = slot_part + dot(activated, w_out, PLAIN)
        grad_part = grad_part + dot(grad_hidden, w_in, WIDTH)
    put_rows(results, 0, slot_part.astype(BF16))
    put_rows(results, 1, grad_part.astype(BF16))


def weight_gradients(group, refs):
    blocks, (act_0, act_1, hid_0, hid_1) = refs[:8], refs[8:12]
    rows, grads = rows_of(blocks, 0), rows_of(blocks, 1)
    hidden = jnp.concatenate([hid_0[group], hid_1[group]], axis=0)
    activated = jnp.concatenate([act_0[group], act_1[group]], axis=0)
    grad_in = dot(rows, hidden, FIRST).astype(BF16)
    return grad_in, dot(activated, grads, FIRST).astype(BF16)


def kept_weight_kernel(side, *refs):
    grad_in, grad_out = refs[12:]
    grad_in[side[0]], grad_out[side[0]] = weight_gradients(0, refs)


def given_weight_kernel(*refs):
    targets = refs[12:]
    target, at = targets[0], 0
    for value in weight_gradients(1, refs):
        rows, columns = value.shape
        for lane in range(0, columns, LANES):
            if at == target.shape[0]:
                target, at = targets[1], 0
            target[at : at + rows, :] = value[:, lane : lane + LANES]
            at += rows


def share_kernel(partials, out):
    total = jnp.sum(partials[...].astype(F32), axis=0).astype(BF16)
    for i in range(out.shape[0]):
        out[i] = total


def by_core(core, first, second):
    return jnp.where(core == 0, first, second), jnp.where(core == 0, second, first)


def router_kernel(
    core, tokens, cotangent, rows, dispatch_in, combine_in, keep, give, grad_logits_out
):
    slots = grad_logits_out.shape[1]
    wide = 2 * slots
    dispatch, combine = dispatch_in[...], combine_in[...]
    inputs = input_columns(dispatch.shape)
    grad_combine = jnp.where(inputs, dot(cotangent[...], rows[...], WIDTH), 0.0)
    grad_dispatch = dot(tokens[...], rows[...], WIDTH)
    logit_combine = combine * (
        grad_combine - jnp.sum(combine * grad_combine, axis=1, keepdims=True)
    )
    logit_dispatch = dispatch * (
        grad_dispatch - jnp.sum(dispatch * grad_dispatch, axis=0, keepdims=True)
    )
    both = logit_combine + pltpu.roll(logit_dispatch, wide - 4, 1)
    both = jnp.where(inputs, both, 0.0).astype(BF16)
    grad_logits = dot(both, spread(slots, wide), WIDTH).astype(BF16)
    grad_logits_out[...] = grad_logits
    term = dot(tokens[...], grad_logits, FIRST)
    kept, given = by_core(core[0], term[: keep.shape[0]], term[keep.shape[0] :])
    keep[...] = kept.astype(BF16)
    give[...] = given.astype(BF16)


def tokens_kernel(rows, router, dispatch_in, combine_in, grad_logits, mixed, grad_tokens):
    inputs = input_columns(dispatch_in.shape)
    combine_b = jnp.where(inputs, combine_in[...], 0.0).astype(BF16)
    dispatch_b = jnp.where(inputs, 0.0, dispatch_in[...]).astype(BF16)
    mixed[...] = dot(combine_b, rows[...], PLAIN).astype(BF16)
    through = dot(dispatch_b, rows[...], PLAIN) + dot(grad_logits[...], router[...], WIDTH)
    grad_tokens[...] = through.astype(BF16)


def pair_kernel(keep, received, out):
    out[...] = add(keep[...], received[...])


def widen_kernel(core, kept, received, out):
    half = out.shape[0] // 2
    kept = kept[...].astype(F32).reshape(half, out.shape[1])
    received = received[...].astype(F32).reshape(half, out.shape[1])
    out[:half, :], out[half:, :] = by_core(core[0], kept, received)


def shape(dims, dtype=BF16):
    return jax.ShapeDtypeStruct(dims, dtype)


def swap(value, axis):
    return lax.all_to_all(value, axis, split_axis=0, concat_axis=0, tiled=True)


def sum_router(keep, give, core, others):
    half, slots = keep.shape
    n_plane = lax.axis_size(PLANE)
    n_z = lax.axis_size("z")
    block = (half // n_plane, slots)
    received = lax.ppermute(give, "c", CORES)
    share = call(pair_kernel, shape(keep.shape), (keep, received), 0, "pair")
    share = swap(share.reshape((n_plane,) + block), PLANE)
    share = call(share_kernel, shape((n_z,) + block), (share,), 0, "share_plane")
    share = swap(share, "z")
    share = call(share_kernel, shape((n_plane,) + block), (share,), 0, "share_z")
    share, others = lax.optimization_barrier((swap(share, PLANE), others))
    received = lax.ppermute(share, "c", CORES)
    full = shape((2 * half, slots), F32)
    return call(widen_kernel, full, (core, share, received), 0, "widen"), others


def per_device(tokens, router, expert_in, expert_out, cotangent):
    n_expert = lax.axis_size(EXPERT)
    count, width = tokens.shape
    slots = router.shape[1]
    wide = 2 * slots
    hidden_units = expert_in.shape[2]
    tied = lax.optimization_barrier
    row, pair = lax.axis_index("yl"), lax.axis_index("yh")
    place = (row + pair) % 2
    side = place.astype(jnp.int32).reshape(1)
    core = lax.axis_index("c").astype(jnp.int32).reshape(1)

    def exchange(value, dim):
        return lax.ppermute(value, DP, neighbour(dim))

    pieces = hidden_units // LANES + width // LANES
    pieces = hidden_units // LANES + width // LANES
    whole = 2 * width * hidden_units // LANES

    def cut(in_pieces, out_pieces):
        first = in_pieces * width + out_pieces * hidden_units
        return shape((first, LANES)), shape((whole - first, LANES))

    copy_sems = (pltpu.SemaphoreType.DMA((pieces,)),)
    packed, packed_late = call(
        pack_kernel,
        cut(3, 3),
        (side, expert_in, expert_out),
        0,
        "pack",
        copy_sems,
        pl.ANY,
    )
    packed, router = tied((packed, router))
    more = exchange(packed, "y1")

    rows, dispatch, combine = call(
        prologue_kernel,
        (shape((wide, width)), shape((count, wide), F32), shape((count, wide), F32)),
        (tokens, router, cotangent),
        6 * count * wide * width,
        "prologue",
    )
    rows = swap(rows.reshape(n_expert, 8, width), EXPERT).reshape(wide, width)
    rows, more = tied((rows, more))
    keep_a, keep_b, give = call(
        sort_kernel,
        (shape((PART, width)), shape((PART, width)), shape((HALF, width))),
        (side, rows),
        2 * wide * wide * width,
        "sort",
    )

    def first_step(a, b):
        a, b = a[None], b[None]
        near_a = jnp.concatenate([a, exchange(a, "x")], axis=0)
        near_b = jnp.concatenate([b, exchange(b, "y3")], axis=0)
        return tied((near_a, near_b))

    def second_step(a, b):
        return a, b, exchange(a, "y3"), exchange(b, "x")

    def experts(blocks, name):
        kept = shape((2, 4 * PART, hidden_units))
        done = call(
            expert_kernel,
            tuple(shape(b.shape) for b in blocks) + (kept, kept),
            (side, *blocks, expert_in, expert_out, more, more_late),
            16 * 4 * PART * width * hidden_units,
            name,
        )
        return done[:4], done[4], done[5]

    taken = exchange(give, "y1")
    packed_late, taken = tied((packed_late, taken))
    more_late = exchange(packed_late, "y1")
    partner = first_step(taken[:PART], taken[PART:])
    own = first_step(keep_a, keep_b)
    partner, own = tied((partner, own))
    partner, own = second_step(*partner), second_step(*own)
    partner_done, partner_act, partner_hid = experts(partner, "experts_partner")
    far_a, far_b, partner_done = tied((own[2], own[3], partner_done))
    own = (own[0], own[1], far_a, far_b)
    own_done, own_act, own_hid = experts(own, "experts_own")

    known = (*own, *partner, own_act, partner_act, own_hid, partner_hid)
    work = 4 * 8 * PART * width * hidden_units
    theirs = call(given_weight_kernel, cut(2, 0), known, work, "weights_given")
    mine = call(
        kept_weight_kernel,
        (shape(expert_in.shape), shape(expert_out.shape)),
        (side, *known),
        work,
        "weights_kept",
    )

    def first_sum(near_a, near_b, far_a, far_b):
        return add(near_a, exchange(far_a, "y3")), add(near_b, exchange(far_b, "x"))

    def second_sum(near_a, near_b, also):
        near_a, near_b, also = tied((near_a, near_b, also))
        arrived_a, arrived_b = exchange(near_a[1], "x"), exchange(near_b[1], "y3")
        return (near_a[0], arrived_a, near_b[0], arrived_b), also

    received = exchange(theirs[0], "y1")
    partner_sum = first_sum(*partner_done)
    partner_sum, own_done = tied((partner_sum, own_done))
    partner_sum, _ = second_sum(*partner_sum, ())
    own_sum, _ = second_sum(*first_sum(*own_done), ())
    a, arrived_a, b, arrived_b = partner_sum
    ready = jnp.concatenate([add(a, arrived_a), add(b, arrived_b)], axis=0)
    ready, received, mine = tied((ready, received, mine))
    returned = exchange(ready, "y1")
    back = call(
        unsort_kernel,
        shape((wide, width)),
        (side, *own_sum, returned),
        2 * wide * wide * width,
        "unsort",
    )
    back, leaving = tied((back, theirs[1]))
    received_late = exchange(leaving, "y1")
    back = swap(back.reshape(n_expert, 8, width), EXPERT).reshape(wide, width)
    keep, give, grad_logits = call(
        router_kernel,
        (shape((width // 2, slots)), shape((width // 2, slots)), shape((count, slots))),
        (core, tokens, cotangent, back, dispatch, combine),
        6 * count * wide * width,
        "router_gradient",
    )
    mixed, grad_tokens = call(
        tokens_kernel,
        (shape((count, width)), shape((count, width))),
        (back, router, dispatch, combine, grad_logits),
        5 * count * wide * width,
        "token_outputs",
    )
    grad_in, grad_out = call(
        merge_kernel,
        (shape(expert_in.shape), shape(expert_out.shape)),
        (side, received, received_late, *mine),
        0,
        "merge",
        copy_sems,
        pl.ANY,
        {3: 0, 4: 1},
    )
    grad_router, others = sum_router(
        keep, give, core, (mixed, grad_tokens, grad_in, grad_out)
    )
    mixed, grad_tokens, grad_in, grad_out = others
    return (mixed, grad_tokens, grad_router, grad_in, grad_out)


def solution(mesh):
    grid = Mesh(mesh.devices.reshape(2, 2, 2, 8, 2, 2), ALL)
    in_specs = (
        P(ALL, None),
        P(),
        P(EXPERT, None, DP),
        P(EXPERT, DP, None),
        P(ALL, None),
    )
    out_specs = (
        P(ALL, None),
        P(ALL, None),
        P(),
        P(EXPERT, None, DP),
        P(EXPERT, DP, None),
    )
    return jax.shard_map(
        per_device, mesh=grid, in_specs=in_specs, out_specs=out_specs, check_vma=False
    )
```
